32 devices in a mesh: group: 2 (over x), route: 4 (over y, core), cuts: 4 (over z).
Axes of the slice: x: 2, y: 2, z: 4, core: 2. Of those that a mesh axis runs over, the one named last changes fastest.
Arguments:
- query_matrix_rows: bfloat16 [1024, 4096], P(('group', 'route'), 'cuts'), parts along dimension 0, may hold values from -8 to 8
- key_matrix_rows: bfloat16 [1024, 1024], P(('group', 'route'), 'cuts'), parts along dimension 0, may hold values from -8 to 8
- value_matrix_rows: bfloat16 [1024, 1024], P(('group', 'route'), 'cuts'), parts along dimension 0, may hold values from -6 to 6
- attention_output_matrix: bfloat16 [4096, 4096], P('cuts'), may hold values from -0.125 to 0.125
- residual: bfloat16 [1024, 4096], P(('group', 'route'), 'cuts'), parts along dimension 0, may hold values from -6 to 6
- cotangent: bfloat16 [1024, 4096], P(('group', 'route'), 'cuts'), parts along dimension 0, may hold values from -0.59765625 to 0.59765625
- token_expert_choices: int32 [1024, 2], P(('group', 'route')), parts along dimension 0, may hold values from 0 to 3, as said below
- token_slot_positions: int32 [1024, 2], P(('group', 'route')), parts along dimension 0, may hold values from 0 to 127, as said below
- router_choice_weight: float32 [1024, 2], P(('group', 'route')), parts along dimension 0, may hold values from 0.2 to 1
- expert_gate_weight: bfloat16 [4, 3200, 4096], P('route', 'cuts'), may hold values from -0.09375 to 0.09375
- expert_down_weight: bfloat16 [4, 3200, 4096], P('route', 'cuts'), may hold values from -0.15625 to 0.15625
- adapter_down_factor: bfloat16 [4, 64, 4096], P('route'), may hold values from -0.09375 to 0.09375
- adapter_up_factor: bfloat16 [4, 64, 3200], P('route', None, 'cuts'), may hold values from -0.75 to 0.75
Outputs:
- layer_out: bfloat16 [1024, 4096], P(('group', 'route'), 'cuts'), parts along dimension 0
- down_factor_gradient: float32 [8, 64, 4096], P(('group', 'route'), None, 'cuts'), parts along dimension 0
- up_factor_gradient: float32 [8, 64, 3200], P(('group', 'route'), None, 'cuts'), parts along dimension 0
The draws below stay inside these ranges and needn't reach their ends.
There are 2 independent parts, one for each index of `group`. The reference program is written for one: setup_inputs(seed, part) draws one part's arguments, and reference() takes and returns one part's arrays. A program takes and returns all parts, laid end to end along the dimension named above; an argument that names none is the same for every part. Nothing has to cross between parts.
Inputs may be any that keep to these rules, and one draw needn't show every extreme that they name: `token_expert_choices`: the two experts of a token differ. Within one sequence of 128 tokens no expert is named more than 128 times; one expert, the same for all sequences of a draw, is named exactly 128 times in every sequence. `token_slot_positions`: within one sequence the slots given for one expert are all different.
All inputs are finite; a program needn't handle non-finite values.
Results may differ from the reference program's by a relative error of at most 0.014.
Values may be sent and summed in bfloat16 or wider, within the bound.
A program may use at most 128 MiB of HBM per device.

```python
import math
import jax
import jax.numpy as jnp
from jax import lax

MODEL_DIMENSION = 4096
HEADS = 32
KV_HEADS = 8
HEAD_DIM = 128
FEEDFORWARD_UNITS = 3200
ADAPTER_RANK = 64
LEN = 128
EXPERT_COUNT = 4
TOKENS = 512
CAP = 128
N_CUTS = 4


def attention_draws(key):
    base_q = jax.random.fold_in(key, 101)
    base_k = jax.random.fold_in(key, 102)
    query_vals = jnp.clip(jax.random.normal(base_q, (TOKENS, HEADS * HEAD_DIM), jnp.float32), -6.0, 6.0)
    key_vals = jnp.clip(jax.random.normal(base_k, (TOKENS, KV_HEADS * HEAD_DIM), jnp.float32), -6.0, 6.0)
    return (query_vals, key_vals)


def draw_query_matrix_rows(key, part):
    return attention_draws(key)[0].astype(jnp.bfloat16)


def draw_key_matrix_rows(key, part):
    return attention_draws(key)[1].astype(jnp.bfloat16)


def routing_draws(key):
    seq_count = TOKENS // LEN
    cell_count = EXPERT_COUNT * CAP
    hot_expert = jax.random.randint(jax.random.fold_in(key, 201), (), 0, EXPERT_COUNT)
    expert_bias = jax.random.randint(jax.random.fold_in(key, 202), (EXPERT_COUNT,), 0, 4 * CAP)

    def per_sequence(seq_key):
        noise_ints = jax.random.randint(jax.random.fold_in(seq_key, 1), (EXPERT_COUNT, CAP), 0, 4 * CAP)
        boost = jnp.where(jnp.arange(EXPERT_COUNT)[:, None] == hot_expert, 16 * CAP, 0)
        scores = noise_ints + expert_bias[:, None] + boost
        unique = scores.reshape(-1) * cell_count + jax.random.permutation(jax.random.fold_in(seq_key, 2), cell_count)
        ranking = jnp.argsort(-unique)
        chosen = jnp.sort(ranking[:2 * LEN])
        first_half = chosen[:LEN]
        second = chosen[LEN:]
        swapped = jax.random.randint(jax.random.fold_in(seq_key, 3), (LEN,), 0, 2) == 1
        paired = jnp.stack([jnp.where(swapped, second, first_half), jnp.where(swapped, first_half, second)], axis=1)
        placing = jax.random.permutation(jax.random.fold_in(seq_key, 4), LEN)
        return paired[jnp.argsort(placing)]
    seq_keys = jax.random.split(jax.random.fold_in(key, 203), seq_count)
    paired = jax.vmap(per_sequence)(seq_keys).reshape(TOKENS, 2)
    return ((paired // CAP).astype(jnp.int32), (paired % CAP).astype(jnp.int32))


def draw_token_expert_choices(key, part):
    return routing_draws(key)[0]


def draw_token_slot_positions(key, part):
    return routing_draws(key)[1]


def strengthened(result, key, source, target, shards_of, factor):
    owner, partner = [(jnp.arange(result.shape[position]) // (result.shape[position] // shards_of)).reshape([-1 if axis == position else 1 for axis in range(result.ndim)]) for position in (source, target)]
    chosen = jax.random.permutation(key, shards_of)[partner]
    strong = (owner == chosen) | (owner == (partner + shards_of // 2) % shards_of)
    return jnp.where(strong, factor * result, result)


def block_scale(key, extent, shards, least, high):
    level = 1.0
    for position, shards_of in shards:
        steps = jax.random.uniform(jax.random.fold_in(jax.random.fold_in(key, 6), position), (shards_of,), jnp.float32, least / len(shards), high / len(shards))
        level = level * jnp.repeat(jnp.exp(steps), extent[position] // shards_of).reshape((-1,) + (1,) * (len(extent) - 1 - position))
    return level


def centred(own_key, dims, deviation, most, cuts=(), kind=jnp.bfloat16):
    values = deviation * jax.random.normal(own_key, dims, jnp.float32)
    if cuts:
        values = values * block_scale(own_key, dims, cuts, -0.22, 0.18)
    return jnp.clip(values, -most, most).astype(kind)


def heavy_noise(own_key, shape, width, limit, pieces, heavy, kind=jnp.bfloat16):
    result = width * jax.random.normal(own_key, shape, jnp.float32)
    if pieces:
        result = result * block_scale(own_key, shape, pieces, -0.22, 0.18)
    return jnp.clip(strengthened(result, jax.random.fold_in(own_key, 3), *heavy), -limit, limit).astype(kind)


def setup_inputs(seed: int = 0, part: int = 0) -> dict:
    arg_keys = jax.random.split(jax.random.key(seed), 14)
    own_keys = jax.random.split(jax.random.fold_in(arg_keys[13], part), 14)
    return {
        "query_matrix_rows": draw_query_matrix_rows(jax.random.fold_in(jax.random.fold_in(arg_keys[13], part), 71), part),
        "key_matrix_rows": draw_key_matrix_rows(jax.random.fold_in(jax.random.fold_in(arg_keys[13], part), 71), part),
        "value_matrix_rows": centred(own_keys[2], (TOKENS, KV_HEADS * HEAD_DIM), 1.0, 6.0, ((0, 4), (1, 4))),
        "attention_output_matrix": heavy_noise(arg_keys[3], (HEADS * HEAD_DIM, MODEL_DIMENSION), (HEADS * HEAD_DIM) ** -0.5, 0.125, ((0, 4),), (0, 1, 4, 2.0)),
        "residual": centred(own_keys[4], (TOKENS, MODEL_DIMENSION), 1.0, 6.0, ((0, 4), (1, 4))),
        "cotangent": centred(own_keys[5], (TOKENS, MODEL_DIMENSION), 0.1, 0.59765625, ((0, 4), (1, 4))),
        "token_expert_choices": draw_token_expert_choices(jax.random.fold_in(jax.random.fold_in(arg_keys[13], part), 71), part),
        "token_slot_positions": draw_token_slot_positions(jax.random.fold_in(jax.random.fold_in(arg_keys[13], part), 71), part),
        "router_choice_weight": jnp.clip(jnp.exp(math.log(1.0) - 1.609438 * jax.random.uniform(own_keys[8], (TOKENS, 2), jnp.float32) ** block_scale(own_keys[8], (TOKENS, 2), ((0, 4),), -0.2, 0.2)), 0.2, 1.0),
        "expert_gate_weight": centred(arg_keys[9], (EXPERT_COUNT, FEEDFORWARD_UNITS, MODEL_DIMENSION), MODEL_DIMENSION ** -0.5, 0.09375, ((0, 4), (1, 4))),
        "expert_down_weight": heavy_noise(arg_keys[10], (EXPERT_COUNT, FEEDFORWARD_UNITS, MODEL_DIMENSION), FEEDFORWARD_UNITS ** -0.5, 0.15625, ((0, 4), (1, 4)), (1, 2, 4, 2.0)),
        "adapter_down_factor": centred(arg_keys[11], (EXPERT_COUNT, ADAPTER_RANK, MODEL_DIMENSION), MODEL_DIMENSION ** -0.5, 0.09375, ((0, 4),)),
        "adapter_up_factor": centred(arg_keys[12], (EXPERT_COUNT, ADAPTER_RANK, FEEDFORWARD_UNITS), ADAPTER_RANK ** -0.5, 0.75, ((0, 4), (2, 4))),
    }


ADAPTER_SCALE = 0.5

def sequence_heads(blocks):
    seq_q, seq_k, seq_v = blocks
    per_kv = HEADS // KV_HEADS
    queries = seq_q.reshape(LEN, KV_HEADS, per_kv, HEAD_DIM).astype(jnp.float32)
    key_view = seq_k.reshape(LEN, KV_HEADS, HEAD_DIM).astype(jnp.float32)
    value_view = seq_v.reshape(LEN, KV_HEADS, HEAD_DIM).astype(jnp.float32)
    scores = jnp.einsum('qhgd,khd->hgqk', queries, key_view) / math.sqrt(HEAD_DIM)
    future = lax.broadcasted_iota(jnp.int32, (LEN, LEN), 1) > lax.broadcasted_iota(jnp.int32, (LEN, LEN), 0)
    scores = jnp.where(future, -jnp.inf, scores)
    row_max = lax.optimization_barrier(jnp.max(scores, axis=-1, keepdims=True))
    shifted = jnp.exp(scores - row_max)
    weights = (shifted / lax.optimization_barrier(jnp.sum(shifted, axis=-1, keepdims=True))).astype(jnp.bfloat16)
    attended = jnp.einsum('hgqk,khd->qhgd', weights.astype(jnp.float32), value_view)
    return attended.astype(jnp.bfloat16).reshape(LEN, HEADS * HEAD_DIM)

def reference(query_matrix_rows, key_matrix_rows, value_matrix_rows, attention_output_matrix, residual, cotangent, token_expert_choices, token_slot_positions, router_choice_weight, expert_gate_weight, expert_down_weight, adapter_down_factor, adapter_up_factor):
    seq_count = TOKENS // LEN
    attended = lax.map(sequence_heads, (query_matrix_rows.reshape(seq_count, LEN, -1), key_matrix_rows.reshape(seq_count, LEN, -1), value_matrix_rows.reshape(seq_count, LEN, -1)))
    attended = attended.reshape(TOKENS, HEADS * HEAD_DIM)
    head_out = jnp.dot(attended, attention_output_matrix, preferred_element_type=jnp.float32)
    hidden = (residual.astype(jnp.float32) + head_out).astype(jnp.bfloat16)
    token_index = jnp.arange(TOKENS, dtype=jnp.int32)
    seq_index = token_index // LEN
    flat_seq = jnp.repeat(seq_index, 2)
    row_pos = (flat_seq * CAP + token_slot_positions.reshape(-1)).astype(jnp.int32)
    owners = jnp.full((EXPERT_COUNT, seq_count * CAP), TOKENS, jnp.int32)
    owners = owners.at[token_expert_choices.reshape(-1), row_pos].set(jnp.repeat(token_index, 2))
    scales = jnp.zeros((EXPERT_COUNT, seq_count * CAP), jnp.float32)
    scales = scales.at[token_expert_choices.reshape(-1), row_pos].set(router_choice_weight.reshape(-1))
    padded_x = jnp.concatenate([hidden, jnp.zeros((1, MODEL_DIMENSION), hidden.dtype)], axis=0)
    padded_g = jnp.concatenate([cotangent, jnp.zeros((1, MODEL_DIMENSION), cotangent.dtype)], axis=0)
    slice_width = FEEDFORWARD_UNITS // N_CUTS

    def expert_step(current_expert):
        expert_input_rows = jnp.take(padded_x, owners[current_expert], axis=0)
        rows_g = (jnp.take(padded_g, owners[current_expert], axis=0).astype(jnp.float32) * scales[current_expert][:, None]).astype(jnp.bfloat16)
        expert_gate_matrix = expert_gate_weight[current_expert]
        down_w = expert_down_weight[current_expert]
        down_factor_slice = adapter_down_factor[current_expert]
        up_factor_slice = adapter_up_factor[current_expert]
        adapter_product = jnp.dot(expert_input_rows, down_factor_slice.T, preferred_element_type=jnp.float32).astype(jnp.bfloat16)
        gate_preactivation = jnp.dot(expert_input_rows, expert_gate_matrix.T, preferred_element_type=jnp.float32) + ADAPTER_SCALE * jnp.dot(adapter_product, up_factor_slice, preferred_element_type=jnp.float32)
        sigmoid_gate = jax.nn.sigmoid(gate_preactivation)
        activ = (gate_preactivation * sigmoid_gate).astype(jnp.bfloat16)
        expert_output_rows = jnp.zeros((expert_input_rows.shape[0], MODEL_DIMENSION), jnp.float32)
        for piece_index in range(N_CUTS):
            lower = piece_index * slice_width
            piece_out = jnp.dot(activ[:, lower:lower + slice_width], down_w[lower:lower + slice_width], preferred_element_type=jnp.float32)
            expert_output_rows = expert_output_rows + piece_out.astype(jnp.bfloat16).astype(jnp.float32)
        grad_hidden = jnp.dot(rows_g, down_w.T, preferred_element_type=jnp.float32)
        preactivation_gradient = (grad_hidden * sigmoid_gate * (1.0 + gate_preactivation * (1.0 - sigmoid_gate))).astype(jnp.bfloat16)
        up_factor_gradient = ADAPTER_SCALE * jnp.dot(adapter_product.T, preactivation_gradient, preferred_element_type=jnp.float32)
        down_factor_gradient = jnp.zeros((ADAPTER_RANK, MODEL_DIMENSION), jnp.float32)
        for piece_index in range(N_CUTS):
            lower = piece_index * slice_width
            factor_part = jnp.dot(preactivation_gradient[:, lower:lower + slice_width], up_factor_slice[:, lower:lower + slice_width].T, preferred_element_type=jnp.float32).astype(jnp.bfloat16)
            down_factor_gradient = down_factor_gradient + jnp.dot(factor_part.T, expert_input_rows, preferred_element_type=jnp.float32)
        return (expert_output_rows, ADAPTER_SCALE * down_factor_gradient, up_factor_gradient)
    outputs, grads_a, grads_b = lax.map(expert_step, jnp.arange(EXPERT_COUNT, dtype=jnp.int32))
    first_out = outputs[token_expert_choices[:, 0], (seq_index * CAP + token_slot_positions[:, 0]).astype(jnp.int32)]
    second_out = outputs[token_expert_choices[:, 1], (seq_index * CAP + token_slot_positions[:, 1]).astype(jnp.int32)]
    picked = router_choice_weight[:, 0:1] * first_out + router_choice_weight[:, 1:2] * second_out
    layer_out = (hidden.astype(jnp.float32) + picked).astype(jnp.bfloat16)
    return (layer_out, grads_a, grads_b)
```

```python
import functools
import math

import jax
import jax.numpy as jnp
from jax import lax
from jax.experimental import pallas as pl
from jax.experimental.pallas import tpu as pltpu
from jax.sharding import PartitionSpec as P

HEAD_DIM = 128


ADAPTER_SCALE = 0.5


def causal_heads(query_matrix_rows, key_matrix_rows, value_matrix_rows):
    length = query_matrix_rows.shape[0]
    kv_local = key_matrix_rows.shape[1] // HEAD_DIM
    per_kv = query_matrix_rows.shape[1] // key_matrix_rows.shape[1]
    queries = query_matrix_rows.reshape(length, kv_local, per_kv, HEAD_DIM)
    key_view = key_matrix_rows.reshape(length, kv_local, HEAD_DIM)
    value_view = value_matrix_rows.reshape(length, kv_local, HEAD_DIM)
    scores = jnp.einsum(
        "qhgd,khd->hgqk", queries, key_view, preferred_element_type=jnp.float32
    ) / math.sqrt(HEAD_DIM)
    future = lax.broadcasted_iota(jnp.int32, (length, length), 1) > lax.broadcasted_iota(
        jnp.int32, (length, length), 0
    )
    scores = jnp.where(future, -jnp.inf, scores)
    row_max = jnp.max(scores, axis=-1, keepdims=True)
    shifted = jnp.exp(scores - row_max)
    weights = (shifted / jnp.sum(shifted, axis=-1, keepdims=True)).astype(jnp.bfloat16)
    attended = jnp.einsum("hgqk,khd->qhgd", weights, value_view, preferred_element_type=jnp.float32)
    return attended.astype(jnp.bfloat16).reshape(length, query_matrix_rows.shape[1])


def fill_slots(source_rows, owners):
    padded = jnp.concatenate(
        [source_rows, jnp.zeros((1, source_rows.shape[1]), source_rows.dtype)], axis=0
    )
    return jnp.take(padded, owners, axis=0)


def weighted_slots(source_rows, owners, scales):
    return (fill_slots(source_rows, owners).astype(jnp.float32) * scales[:, None]).astype(
        jnp.bfloat16
    )


def combine_rows(returned, cell_ids, router_choice_weight):
    first_out = jnp.take(returned, cell_ids[:, 0], axis=0)
    second_out = jnp.take(returned, cell_ids[:, 1], axis=0)
    return router_choice_weight[:, 0:1] * first_out + router_choice_weight[:, 1:2] * second_out


def exchanged_slots(
    query_matrix_rows,
    key_matrix_rows,
    value_matrix_rows,
    attention_output_matrix,
    residual,
    cotangent,
    token_expert_choices,
    token_slot_positions,
    router_choice_weight,
    expert_gate_weight,
    expert_down_weight,
    adapter_down_factor,
    adapter_up_factor,
):
    attended = causal_heads(query_matrix_rows, key_matrix_rows, value_matrix_rows)
    head_terms = jnp.dot(attended, attention_output_matrix, preferred_element_type=jnp.float32)
    head_cols = lax.psum_scatter(head_terms, "cuts", scatter_dimension=1, tiled=True)
    hidden_cols = (residual.astype(jnp.float32) + head_cols).astype(jnp.bfloat16)
    length = residual.shape[0]
    col_count = residual.shape[1]
    model_width = expert_gate_weight.shape[2]
    experts = lax.axis_size("route")
    capacity = 4 * length // experts
    cell_ids = token_expert_choices * capacity + token_slot_positions
    flat_cells = cell_ids.reshape(-1)
    owners = (
        jnp.full((experts * capacity,), length, jnp.int32)
        .at[flat_cells]
        .set(jnp.repeat(jnp.arange(length, dtype=jnp.int32), 2))
    )
    scales = (
        jnp.zeros((experts * capacity,), jnp.float32)
        .at[flat_cells]
        .set(router_choice_weight.reshape(-1))
    )
    full_x, full_g = (
        lax.all_gather(hidden_cols, "cuts", axis=1, tiled=True),
        lax.all_gather(cotangent, "cuts", axis=1, tiled=True),
    )
    token_part = fill_slots(full_x, owners).reshape(experts, capacity, model_width)
    grad_part = weighted_slots(full_g, owners, scales).reshape(experts, capacity, model_width)
    slot_x, slot_g = (
        lax.all_to_all(token_part, "route", split_axis=0, concat_axis=0, tiled=True),
        lax.all_to_all(grad_part, "route", split_axis=0, concat_axis=0, tiled=True),
    )
    expert_input_rows = slot_x.reshape(-1, model_width)
    rows_g = slot_g.reshape(-1, model_width)
    reduce_final_axis = (((1,), (1,)), ((), ()))
    contract_first = (((0,), (0,)), ((), ()))
    gate_primary_product = lax.dot_general(
        expert_input_rows,
        expert_gate_weight[0],
        reduce_final_axis,
        preferred_element_type=jnp.float32,
    )
    adapter_product = lax.dot_general(
        expert_input_rows,
        adapter_down_factor[0],
        reduce_final_axis,
        preferred_element_type=jnp.float32,
    ).astype(jnp.bfloat16)
    gate_preactivation = gate_primary_product + ADAPTER_SCALE * jnp.dot(
        adapter_product, adapter_up_factor[0], preferred_element_type=jnp.float32
    )
    sigmoid_gate = jax.nn.sigmoid(gate_preactivation)
    activ = (gate_preactivation * sigmoid_gate).astype(jnp.bfloat16)
    partial_out = jnp.dot(activ, expert_down_weight[0], preferred_element_type=jnp.float32).astype(
        jnp.bfloat16
    )
    slot_sums = lax.psum_scatter(
        partial_out.astype(jnp.float32)
        .reshape(experts, capacity, model_width)
        .astype(jnp.bfloat16),
        "cuts",
        scatter_dimension=2,
        tiled=True,
    ).astype(jnp.float32)
    returned = (
        lax.all_to_all(
            slot_sums.astype(jnp.bfloat16), "route", split_axis=0, concat_axis=0, tiled=True
        )
        .astype(slot_sums.dtype)
        .reshape(experts * capacity, col_count)
    )
    merged = hidden_cols.astype(jnp.float32) + combine_rows(
        returned, cell_ids, router_choice_weight
    )
    layer_out = merged.astype(jnp.bfloat16)
    grad_hidden = lax.dot_general(
        rows_g, expert_down_weight[0], reduce_final_axis, preferred_element_type=jnp.float32
    )
    preactivation_gradient = (
        grad_hidden * sigmoid_gate * (1.0 + gate_preactivation * (1.0 - sigmoid_gate))
    ).astype(jnp.bfloat16)
    up_factor_gradient = ADAPTER_SCALE * lax.dot_general(
        adapter_product, preactivation_gradient, contract_first, preferred_element_type=jnp.float32
    )
    factor_part = lax.dot_general(
        preactivation_gradient,
        adapter_up_factor[0],
        reduce_final_axis,
        preferred_element_type=jnp.float32,
    ).astype(jnp.bfloat16)
    gradient_pieces = lax.dot_general(
        factor_part, expert_input_rows, contract_first, preferred_element_type=jnp.float32
    )
    down_factor_gradient = ADAPTER_SCALE * lax.psum_scatter(
        gradient_pieces.astype(jnp.bfloat16), "cuts", scatter_dimension=1, tiled=True
    ).astype(jnp.float32)
    return (layer_out, down_factor_gradient[None], up_factor_gradient[None])


MESH = pl.DeviceIdType.MESH
NT = (((1,), (1,)), ((), ()))
VMEM_GRANT = 60 * 2**20


def fused_kernel(
    n_r,
    n_c,
    q_ref,
    k_ref,
    v_ref,
    res_ref,
    cot_ref,
    wt_ref,
    adn_ref,
    aup_ref,
    wo_hbm,
    gate_hbm,
    down_hbm,
    out_ref,
    dgrad_ref,
    ugrad_ref,
    wo,
    gate,
    down,
    xbuf,
    gbuf,
    part,
    rs_in,
    opart,
    core_in,
    y_in,
    oz_in,
    acc_p,
    acc_g,
    low,
    act,
    gpre,
    att,
    hid,
    fac,
    wbuf,
    wcol,
    load_sem,
    ag_send,
    ag_recv,
    rs_send,
    rs_recv,
    core_send,
    core_recv,
    y_send,
    y_recv,
    oz_send,
    oz_recv,
    f_send,
    f_recv,
    w_send,
    w_recv,
):
    f32 = jnp.float32
    bf16 = jnp.bfloat16
    grp = lax.axis_index("group")
    r = lax.axis_index("route")
    c = lax.axis_index("cuts")
    core = r % 2
    chip = r // 2
    r_core = chip * 2 + (1 - core)
    r_y = (1 - chip) * 2 + core
    r_diag = (1 - chip) * 2 + (1 - core)
    rows, cols = res_ref.shape

    def rslice(s):
        return pl.ds(pl.multiple_of(s * rows, rows), rows)

    def cslice(j):
        return pl.ds(pl.multiple_of(j * cols, cols), cols)

    def remote(src, dst, ss, rs, dr, dc):
        return pltpu.make_async_remote_copy(
            src_ref=src,
            dst_ref=dst,
            send_sem=ss,
            recv_sem=rs,
            device_id=(grp, dr, dc),
            device_id_type=MESH,
        )

    barrier = pltpu.get_barrier_semaphore()
    for d in range(1, n_r):
        pl.semaphore_signal(
            barrier, inc=1, device_id=(grp, (r + d) % n_r, c), device_id_type=MESH
        )
    for d in range(1, n_c):
        pl.semaphore_signal(
            barrier, inc=1, device_id=(grp, r, (c + d) % n_c), device_id_type=MESH
        )

    def slot_of(t):
        k = n_c - 1 - t // 2
        j = jnp.where(t % 2 == 0, c + k, c - k)
        return k, j, (j >= 0) & (j < n_c) & ((k > 0) | (t % 2 == 0))

    n_slots = 2 * n_c - 1

    def wo_copy(j):
        return pltpu.make_async_copy(
            wo_hbm.at[:, cslice(j)], wo.at[:, cslice(j)], load_sem.at[j]
        )

    def each_slot(body):
        def step(t, carry):
            k, j, ok = slot_of(t)

            @pl.when(ok)
            def _():
                body(k, j)

            return carry

        lax.fori_loop(0, n_slots, step, 0)

    each_slot(lambda k, j: wo_copy(j).start())
    down_copy = pltpu.make_async_copy(down_hbm, down, load_sem.at[n_c])
    gate_copy = pltpu.make_async_copy(gate_hbm, gate, load_sem.at[n_c + 1])
    down_copy.start()
    gate_copy.start()

    gbuf[c, rslice(r)] = cot_ref[...]
    wbuf[r] = wt_ref[...]
    pl.semaphore_wait(barrier, n_r - 1 + n_c - 1)

    def ag(kind, buf, what, j, s, dr, dc):
        place = buf.at[j, rslice(s)]
        return remote(
            place, place, ag_send.at[kind, what, j], ag_recv.at[kind, j, s], dr, dc
        )

    def up(kind, buf, j):
        return ag(kind, buf, 0, j, r, r, jnp.minimum(c + 1, n_c - 1))

    def dn(kind, buf, j):
        return ag(kind, buf, 1, j, r, r, jnp.maximum(c - 1, 0))

    def across(kind, buf, j):
        return ag(kind, buf, 2, j, r, r_y, c)

    def own_core(kind, buf, j):
        return ag(kind, buf, 3, j, r, r_core, c)

    def fwd_core(kind, buf, j):
        return ag(kind, buf, 4, j, r_y, r_core, c)

    def arrived(kind, buf, j, s):
        ag(kind, buf, 0, j, s, r_core, c).wait_recv()

    def spread(kind, buf, j):
        across(kind, buf, j).start()

        @pl.when((j <= c) & (c < n_c - 1))
        def _():
            up(kind, buf, j).start()

        @pl.when((j >= c) & (c > 0))
        def _():
            dn(kind, buf, j).start()

        own_core(kind, buf, j).start()

    def both_sides(k, body):
        @pl.when(c - k >= 0)
        def _():
            body(c - k)

        @pl.when((c + k < n_c) & (k > 0))
        def _():
            body(c + k)

    def z_stage(kind, buf, k):
        def one(j):
            arrived(kind, buf, j, r)
            spread(kind, buf, j)

        both_sides(k, one)

    def y_stage(kind, buf, k):
        def one(j):
            arrived(kind, buf, j, r_y)
            fwd_core(kind, buf, j).start()

        both_sides(k, one)

    def c_stage(kind, buf, k, body):
        def step(side, carry):
            j = jnp.where(side == 0, c - k, c + k)

            @pl.when((j >= 0) & (j < n_c) & ((k > 0) | (side == 0)))
            def _():
                arrived(kind, buf, j, r_core)
                arrived(kind, buf, j, r_diag)
                body(j)

            return carry

        lax.fori_loop(0, 2, step, 0)

    def ag_finish(kind, buf):
        def step(j, carry):
            across(kind, buf, j).wait_send()

            @pl.when((j <= c) & (c < n_c - 1))
            def _():
                up(kind, buf, j).wait_send()

            @pl.when((j >= c) & (c > 0))
            def _():
                dn(kind, buf, j).wait_send()

            own_core(kind, buf, j).wait_send()
            fwd_core(kind, buf, j).wait_send()
            return carry

        lax.fori_loop(0, n_c, step, 0)

    spread(0, gbuf, c)

    def w_copy(d):
        return remote(
            wbuf.at[r], wbuf.at[r], w_send.at[d], w_recv.at[r], (r + d) % n_r, c
        )

    for d in range(1, n_r):
        w_copy(d).start()

    kv_heads = k_ref.shape[1] // HEAD_DIM
    heads = q_ref.shape[1] // HEAD_DIM
    future = lax.broadcasted_iota(jnp.int32, (rows, rows), 1) > lax.broadcasted_iota(
        jnp.int32, (rows, rows), 0
    )
    for h in range(heads):
        g = h // (heads // kv_heads)
        sc = lax.dot_general(
            q_ref[:, h * HEAD_DIM : (h + 1) * HEAD_DIM],
            k_ref[:, g * HEAD_DIM : (g + 1) * HEAD_DIM],
            NT,
            preferred_element_type=f32,
        ) / math.sqrt(HEAD_DIM)
        sc = jnp.where(future, -jnp.inf, sc)
        ex = jnp.exp(sc - jnp.max(sc, axis=-1, keepdims=True))
        wts = (ex / jnp.sum(ex, axis=-1, keepdims=True)).astype(bf16)
        att[:, h * HEAD_DIM : (h + 1) * HEAD_DIM] = jnp.dot(
            wts,
            v_ref[:, g * HEAD_DIM : (g + 1) * HEAD_DIM],
            preferred_element_type=f32,
        ).astype(bf16)

    def line_copy(buf_at, inbox, ss, rs, j, upward):
        dc = jnp.minimum(c + 1, n_c - 1) if upward else jnp.maximum(c - 1, 0)
        side = 0 if upward else 1
        return remote(buf_at(j), inbox.at[side, j], ss.at[j], rs.at[side, j], r, dc)

    def line_step(buf_at, load, store, inbox, ss, rs, j):
        @pl.when(j > c)
        def _():
            @pl.when(c > 0)
            def _():
                line_copy(buf_at, inbox, ss, rs, j, True).wait_recv()
                store(j, load(j) + inbox[0, j].astype(f32))

            line_copy(buf_at, inbox, ss, rs, j, True).start()

        @pl.when(j < c)
        def _():
            @pl.when(c < n_c - 1)
            def _():
                line_copy(buf_at, inbox, ss, rs, j, False).wait_recv()
                store(j, load(j) + inbox[1, j].astype(f32))

            line_copy(buf_at, inbox, ss, rs, j, False).start()

    def line_final(buf_at, inbox, ss, rs, total):
        @pl.when(c > 0)
        def _():
            line_copy(buf_at, inbox, ss, rs, c, True).wait_recv()
            total[...] += inbox[0, c].astype(f32)

        @pl.when(c < n_c - 1)
        def _():
            line_copy(buf_at, inbox, ss, rs, c, False).wait_recv()
            total[...] += inbox[1, c].astype(f32)

    def line_finish(buf_at, inbox, ss, rs):
        def step(j, carry):
            @pl.when(j != c)
            def _():
                line_copy(buf_at, inbox, ss, rs, j, True).wait_send()

            return carry

        lax.fori_loop(0, n_c, step, 0)

    def part_at(j):
        return part.at[j]

    def part_load(j):
        return part[j].astype(f32)

    def part_store(j, value):
        part[j] = value.astype(bf16)

    def project(j):
        wo_copy(j).wait()
        return jnp.dot(att[...], wo[:, cslice(j)], preferred_element_type=f32)

    def rs_loop(i, carry):
        k = n_c - 1 - i

        def side_step(side, carry2):
            j = jnp.where(side == 0, c + k, c - k)

            @pl.when((j >= 0) & (j < n_c))
            def _():
                part[j] = project(j).astype(bf16)
                line_step(part_at, part_load, part_store, rs_in, rs_send, rs_recv, j)

            return carry2

        lax.fori_loop(0, 2, side_step, 0)
        z_stage(0, gbuf, i + 1)
        y_stage(0, gbuf, i)
        return carry

    lax.fori_loop(0, n_c - 1, rs_loop, 0)
    hid[...] = res_ref[...].astype(f32) + project(c)
    line_final(part_at, rs_in, rs_send, rs_recv, hid)
    xbuf[c, rslice(r)] = hid[...].astype(bf16)
    spread(1, xbuf, c)
    y_stage(0, gbuf, n_c - 1)

    acc_p[...] = jnp.zeros_like(acc_p)
    acc_g[...] = jnp.zeros_like(acc_g)
    low[...] = jnp.zeros_like(low)
    half = 2 * rows
    n_half = n_r // 2

    def grad_mm(j):
        def step(m, carry):
            at = pl.ds(pl.multiple_of(m * half, half), half)
            acc_g[at] += lax.dot_general(
                gbuf[j, at], down[:, cslice(j)], NT, preferred_element_type=f32
            )
            return carry

        lax.fori_loop(0, n_half, step, 0)

    def gate_mm(j):
        def step(m, carry):
            at = pl.ds(pl.multiple_of(m * half, half), half)
            x = xbuf[j, at]
            acc_p[at] += lax.dot_general(
                x, gate[:, cslice(j)], NT, preferred_element_type=f32
            )
            low[at] += lax.dot_general(
                x, adn_ref[:, cslice(j)], NT, preferred_element_type=f32
            )
            return carry

        lax.fori_loop(0, n_half, step, 0)

    down_copy.wait()
    gate_copy.wait()

    def hidden_loop(i, carry):
        @pl.when(i <= n_c - 2)
        def _():
            z_stage(1, xbuf, i + 1)

        @pl.when(i <= n_c - 1)
        def _():
            c_stage(0, gbuf, i, grad_mm)
            y_stage(1, xbuf, i)

        @pl.when(i >= 1)
        def _():
            c_stage(1, xbuf, i - 1, gate_mm)

        return carry

    lax.fori_loop(0, n_c + 1, hidden_loop, 0)

    for d in range(1, n_r):
        src = (r + d) % n_r
        remote(
            wbuf.at[src], wbuf.at[src], w_send.at[d], w_recv.at[src], src, c
        ).wait_recv()

    eye = lax.broadcasted_iota(jnp.int32, (rows, rows), 1) == lax.broadcasted_iota(
        jnp.int32, (rows, rows), 0
    )
    mine = lax.broadcasted_iota(jnp.int32, wt_ref.shape, 0) == r

    def act_step(i, carry):
        s = (1 - chip) * 2 + i
        s = jnp.where(s >= n_r, s - n_r, s)
        at = rslice(s)
        w_row = jnp.sum(jnp.where(mine, wbuf[s], 0.0), axis=0, keepdims=True)
        w = jnp.sum(jnp.where(eye, w_row, 0.0), axis=1, keepdims=True)
        wcol[at] = jnp.broadcast_to(w, (rows, wcol.shape[1]))
        z = acc_p[at] + ADAPTER_SCALE * jnp.dot(
            low[at].astype(bf16), aup_ref[...], preferred_element_type=f32
        )
        sig = 1.0 / (1.0 + jnp.exp(-z))
        act[at] = (z * sig).astype(bf16)
        gpre[at] = (acc_g[at] * w * (sig * (1.0 + z * (1.0 - sig)))).astype(bf16)
        return carry

    lax.fori_loop(0, n_r, act_step, 0)

    def out_mm(j, base):
        at = pl.ds(pl.multiple_of(base * rows, rows), half)
        prod = jnp.dot(act[at], down[:, cslice(j)], preferred_element_type=f32)
        opart[j, at] = (prod * wcol[at, 0:1]).astype(bf16)

    def core_copy(which, j, s):
        return remote(
            opart.at[j, rslice(s)],
            core_in.at[which, j],
            core_send.at[which, j],
            core_recv.at[which, j],
            r_core,
            c,
        )

    def y_copy(j):
        return remote(
            opart.at[j, rslice(r_y)], y_in.at[j], y_send.at[j], y_recv.at[j], r_y, c
        )

    def other_mm(k, j):
        out_mm(j, (1 - chip) * 2)
        core_copy(0, j, r_diag).start()

    def other_pair(k, j):
        core_copy(0, j, r_diag).wait_recv()
        at = rslice(r_y)
        opart[j, at] = (opart[j, at].astype(f32) + core_in[0, j].astype(f32)).astype(bf16)
        y_copy(j).start()

    def other_loop(t, carry):
        k, j, ok = slot_of(t)

        @pl.when(ok & (t < n_slots))
        def _():
            other_mm(k, j)

        k1, j1, ok1 = slot_of(t - 1)

        @pl.when(ok1 & (t > 0))
        def _():
            other_pair(k1, j1)

        return carry

    lax.fori_loop(0, n_slots + 1, other_loop, 0)

    fac[c] = lax.dot_general(
        aup_ref[...], gpre[...], NT, preferred_element_type=f32
    ).astype(bf16)

    def f_copy(d, owner):
        return remote(
            fac.at[owner], fac.at[owner], f_send.at[d], f_recv.at[owner], r, (c + d) % n_c
        )

    for d in range(1, n_c):
        f_copy(d, c).start()

    def own_mm(k, j):
        out_mm(j, chip * 2)
        core_copy(1, j, r_core).start()

    each_slot(own_mm)

    ugrad_ref[...] = ADAPTER_SCALE * jnp.dot(
        low[...].T.astype(bf16), gpre[...], preferred_element_type=f32
    )
    for d in range(1, n_c):
        f_copy(d, (c + d) % n_c).wait_recv()
    total_f = fac[0].astype(f32)
    for d in range(1, n_c):
        total_f = total_f + fac[d].astype(f32)
    dgrad_ref[...] = ADAPTER_SCALE * jnp.dot(
        total_f.astype(bf16), xbuf[c], preferred_element_type=f32
    )

    def out_at(j):
        return opart.at[j, rslice(r)]

    def out_load(j):
        return opart[j, rslice(r)].astype(f32)

    def out_store(j, value):
        opart[j, rslice(r)] = value.astype(bf16)

    def route_total(j):
        core_copy(1, j, r_core).wait_recv()
        y_copy(j).wait_recv()
        return out_load(j) + core_in[1, j].astype(f32) + y_in[j].astype(f32)

    def reduce_step(k, j):
        @pl.when(k > 0)
        def _():
            out_store(j, route_total(j))
            line_step(out_at, out_load, out_store, oz_in, oz_send, oz_recv, j)

    each_slot(reduce_step)
    hid[...] = xbuf[c, rslice(r)].astype(f32) + route_total(c)
    line_final(out_at, oz_in, oz_send, oz_recv, hid)
    out_ref[...] = hid[...].astype(bf16)

    ag_finish(0, gbuf)
    ag_finish(1, xbuf)
    line_finish(part_at, rs_in, rs_send, rs_recv)
    line_finish(out_at, oz_in, oz_send, oz_recv)
    for d in range(1, n_r):
        w_copy(d).wait_send()
    for d in range(1, n_c):
        f_copy(d, c).wait_send()

    def last(j, carry):
        core_copy(0, j, r_diag).wait_send()
        core_copy(1, j, r_core).wait_send()
        y_copy(j).wait_send()
        return carry

    lax.fori_loop(0, n_c, last, 0)


def scratch_list(n_r, n_c, rows, cols, inner, units, rank, w_rows):
    bf16 = jnp.bfloat16
    f32 = jnp.float32
    dma = pltpu.SemaphoreType.DMA
    width = n_c * cols
    tokens = n_r * rows
    return [
        pltpu.VMEM((inner, width), bf16),
        pltpu.VMEM((units, width), bf16),
        pltpu.VMEM((units, width), bf16),
        pltpu.VMEM((n_c, tokens, cols), bf16),
        pltpu.VMEM((n_c, tokens, cols), bf16),
        pltpu.VMEM((n_c, rows, cols), bf16),
        pltpu.VMEM((2, n_c, rows, cols), bf16),
        pltpu.VMEM((n_c, tokens, cols), bf16),
        pltpu.VMEM((2, n_c, rows, cols), bf16),
        pltpu.VMEM((n_c, rows, cols), bf16),
        pltpu.VMEM((2, n_c, rows, cols), bf16),
        pltpu.VMEM((tokens, units), f32),
        pltpu.VMEM((tokens, units), f32),
        pltpu.VMEM((tokens, rank), f32),
        pltpu.VMEM((tokens, units), bf16),
        pltpu.VMEM((tokens, units), bf16),
        pltpu.VMEM((rows, inner), bf16),
        pltpu.VMEM((rows, cols), f32),
        pltpu.VMEM((n_c, rank, tokens), bf16),
        pltpu.VMEM((n_r, w_rows, rows), f32),
        pltpu.VMEM((tokens, 128), f32),
        dma((n_c + 2,)),
        dma((2, 5, n_c)),
        dma((2, n_c, n_r)),
        dma((n_c,)),
        dma((2, n_c)),
        dma((2, n_c)),
        dma((2, n_c)),
        dma((n_c,)),
        dma((n_c,)),
        dma((n_c,)),
        dma((2, n_c)),
        dma((n_c,)),
        dma((n_c,)),
        dma((n_r,)),
        dma((n_r,)),
    ]


def dense_tokens(n_r, n_c, *args):
    (q, k, v, wo, res, cot, choices, _, router, gate, down, adn, aup) = args
    rows, cols = res.shape
    units = gate.shape[1]
    rank = adn.shape[1]
    w_rows = -(-n_r // 8) * 8
    hits = choices.T[:, None, :] == jnp.arange(w_rows, dtype=jnp.int32)[None, :, None]
    wt = jnp.sum(jnp.where(hits, router.T[:, None, :], 0.0), axis=0)
    vmem = pl.BlockSpec(memory_space=pltpu.VMEM)
    hbm = pl.BlockSpec(memory_space=pltpu.HBM)
    tokens = n_r * rows
    outs = pl.pallas_call(
        functools.partial(fused_kernel, n_r, n_c),
        out_shape=(
            jax.ShapeDtypeStruct((rows, cols), jnp.bfloat16),
            jax.ShapeDtypeStruct((rank, cols), jnp.float32),
            jax.ShapeDtypeStruct((rank, units), jnp.float32),
        ),
        in_specs=[vmem] * 8 + [hbm] * 3,
        out_specs=(vmem, vmem, vmem),
        scratch_shapes=scratch_list(
            n_r, n_c, rows, cols, q.shape[1], units, rank, w_rows
        ),
        compiler_params=pltpu.CompilerParams(
            collective_id=0, has_side_effects=True, vmem_limit_bytes=VMEM_GRANT
        ),
        cost_estimate=pl.CostEstimate(
            flops=6 * tokens * units * cols * n_c,
            bytes_accessed=2 * (q.shape[1] + 2 * units) * cols * n_c,
            transcendentals=tokens * units,
        ),
    )(q, k, v, res, cot, wt, adn[0], aup[0], wo, gate[0], down[0])
    return outs[0], outs[1][None], outs[2][None]


def local(n_r, n_c, *args):
    length = args[4].shape[0]
    capacity = 4 * length // n_r
    if capacity == length and n_r == 2 * 2:
        return dense_tokens(n_r, n_c, *args)
    return exchanged_slots(*args)


def solution(mesh):
    return jax.shard_map(
        functools.partial(local, mesh.shape["route"], mesh.shape["cuts"]),
        mesh=mesh,
        in_specs=(
            P(("group", "route"), "cuts"),
            P(("group", "route"), "cuts"),
            P(("group", "route"), "cuts"),
            P("cuts", None),
            P(("group", "route"), "cuts"),
            P(("group", "route"), "cuts"),
            P(("group", "route"), None),
            P(("group", "route"), None),
            P(("group", "route"), None),
            P("route", "cuts", None),
            P("route", "cuts", None),
            P("route", None, None),
            P("route", None, "cuts"),
        ),
        out_specs=(
            P(("group", "route"), "cuts"),
            P(("group", "route"), None, "cuts"),
            P(("group", "route"), None, "cuts"),
        ),
        check_vma=False,
    )
```

```python
import functools
import math

import jax
import jax.numpy as jnp
from jax import lax
from jax.experimental import pallas as pl
from jax.experimental.pallas import tpu as pltpu
from jax.sharding import PartitionSpec as P

HEAD_DIM = 128


ADAPTER_SCALE = 0.5


def causal_heads(query_matrix_rows, key_matrix_rows, value_matrix_rows):
    length = query_matrix_rows.shape[0]
    kv_local = key_matrix_rows.shape[1] // HEAD_DIM
    per_kv = query_matrix_rows.shape[1] // key_matrix_rows.shape[1]
    queries = query_matrix_rows.reshape(length, kv_local, per_kv, HEAD_DIM)
    key_view = key_matrix_rows.reshape(length, kv_local, HEAD_DIM)
    value_view = value_matrix_rows.reshape(length, kv_local, HEAD_DIM)
    scores = jnp.einsum(
        "qhgd,khd->hgqk", queries, key_view, preferred_element_type=jnp.float32
    ) / math.sqrt(HEAD_DIM)
    future = lax.broadcasted_iota(jnp.int32, (length, length), 1) > lax.broadcasted_iota(
        jnp.int32, (length, length), 0
    )
    scores = jnp.where(future, -jnp.inf, scores)
    row_max = jnp.max(scores, axis=-1, keepdims=True)
    shifted = jnp.exp(scores - row_max)
    weights = (shifted / jnp.sum(shifted, axis=-1, keepdims=True)).astype(jnp.bfloat16)
    attended = jnp.einsum("hgqk,khd->qhgd", weights, value_view, preferred_element_type=jnp.float32)
    return attended.astype(jnp.bfloat16).reshape(length, query_matrix_rows.shape[1])


def fill_slots(source_rows, owners):
    padded = jnp.concatenate(
        [source_rows, jnp.zeros((1, source_rows.shape[1]), source_rows.dtype)], axis=0
    )
    return jnp.take(padded, owners, axis=0)


def weighted_slots(source_rows, owners, scales):
    return (fill_slots(source_rows, owners).astype(jnp.float32) * scales[:, None]).astype(
        jnp.bfloat16
    )


def combine_rows(returned, cell_ids, router_choice_weight):
    first_out = jnp.take(returned, cell_ids[:, 0], axis=0)
    second_out = jnp.take(returned, cell_ids[:, 1], axis=0)
    return router_choice_weight[:, 0:1] * first_out + router_choice_weight[:, 1:2] * second_out


def exchanged_slots(
    query_matrix_rows,
    key_matrix_rows,
    value_matrix_rows,
    attention_output_matrix,
    residual,
    cotangent,
    token_expert_choices,
    token_slot_positions,
    router_choice_weight,
    expert_gate_weight,
    expert_down_weight,
    adapter_down_factor,
    adapter_up_factor,
):
    attended = causal_heads(query_matrix_rows, key_matrix_rows, value_matrix_rows)
    head_terms = jnp.dot(attended, attention_output_matrix, preferred_element_type=jnp.float32)
    head_cols = lax.psum_scatter(head_terms, "cuts", scatter_dimension=1, tiled=True)
    hidden_cols = (residual.astype(jnp.float32) + head_cols).astype(jnp.bfloat16)
    length = residual.shape[0]
    col_count = residual.shape[1]
    model_width = expert_gate_weight.shape[2]
    experts = lax.axis_size("route")
    capacity = 4 * length // experts
    cell_ids = token_expert_choices * capacity + token_slot_positions
    flat_cells = cell_ids.reshape(-1)
    owners = (
        jnp.full((experts * capacity,), length, jnp.int32)
        .at[flat_cells]
        .set(jnp.repeat(jnp.arange(length, dtype=jnp.int32), 2))
    )
    scales = (
        jnp.zeros((experts * capacity,), jnp.float32)
        .at[flat_cells]
        .set(router_choice_weight.reshape(-1))
    )
    full_x, full_g = (
        lax.all_gather(hidden_cols, "cuts", axis=1, tiled=True),
        lax.all_gather(cotangent, "cuts", axis=1, tiled=True),
    )
    token_part = fill_slots(full_x, owners).reshape(experts, capacity, model_width)
    grad_part = weighted_slots(full_g, owners, scales).reshape(experts, capacity, model_width)
    slot_x, slot_g = (
        lax.all_to_all(token_part, "route", split_axis=0, concat_axis=0, tiled=True),
        lax.all_to_all(grad_part, "route", split_axis=0, concat_axis=0, tiled=True),
    )
    expert_input_rows = slot_x.reshape(-1, model_width)
    rows_g = slot_g.reshape(-1, model_width)
    reduce_final_axis = (((1,), (1,)), ((), ()))
    contract_first = (((0,), (0,)), ((), ()))
    gate_primary_product = lax.dot_general(
        expert_input_rows,
        expert_gate_weight[0],
        reduce_final_axis,
        preferred_element_type=jnp.float32,
    )
    adapter_product = lax.dot_general(
        expert_input_rows,
        adapter_down_factor[0],
        reduce_final_axis,
        preferred_element_type=jnp.float32,
    ).astype(jnp.bfloat16)
    gate_preactivation = gate_primary_product + ADAPTER_SCALE * jnp.dot(
        adapter_product, adapter_up_factor[0], preferred_element_type=jnp.float32
    )
    sigmoid_gate = jax.nn.sigmoid(gate_preactivation)
    activ = (gate_preactivation * sigmoid_gate).astype(jnp.bfloat16)
    partial_out = jnp.dot(activ, expert_down_weight[0], preferred_element_type=jnp.float32).astype(
        jnp.bfloat16
    )
    slot_sums = lax.psum_scatter(
        partial_out.astype(jnp.float32)
        .reshape(experts, capacity, model_width)
        .astype(jnp.bfloat16),
        "cuts",
        scatter_dimension=2,
        tiled=True,
    ).astype(jnp.float32)
    returned = (
        lax.all_to_all(
            slot_sums.astype(jnp.bfloat16), "route", split_axis=0, concat_axis=0, tiled=True
        )
        .astype(slot_sums.dtype)
        .reshape(experts * capacity, col_count)
    )
    merged = hidden_cols.astype(jnp.float32) + combine_rows(
        returned, cell_ids, router_choice_weight
    )
    layer_out = merged.astype(jnp.bfloat16)
    grad_hidden = lax.dot_general(
        rows_g, expert_down_weight[0], reduce_final_axis, preferred_element_type=jnp.float32
    )
    preactivation_gradient = (
        grad_hidden * sigmoid_gate * (1.0 + gate_preactivation * (1.0 - sigmoid_gate))
    ).astype(jnp.bfloat16)
    up_factor_gradient = ADAPTER_SCALE * lax.dot_general(
        adapter_product, preactivation_gradient, contract_first, preferred_element_type=jnp.float32
    )
    factor_part = lax.dot_general(
        preactivation_gradient,
        adapter_up_factor[0],
        reduce_final_axis,
        preferred_element_type=jnp.float32,
    ).astype(jnp.bfloat16)
    gradient_pieces = lax.dot_general(
        factor_part, expert_input_rows, contract_first, preferred_element_type=jnp.float32
    )
    down_factor_gradient = ADAPTER_SCALE * lax.psum_scatter(
        gradient_pieces.astype(jnp.bfloat16), "cuts", scatter_dimension=1, tiled=True
    ).astype(jnp.float32)
    return (layer_out, down_factor_gradient[None], up_factor_gradient[None])


MESH = pl.DeviceIdType.MESH
NT = (((1,), (1,)), ((), ()))
VMEM_GRANT = 60 * 2**20
AHEAD = 1


def fused_kernel(
    n_r,
    n_c,
    q_ref,
    k_ref,
    v_ref,
    res_ref,
    cot_ref,
    wt_ref,
    adn_ref,
    aup_ref,
    wo_hbm,
    gate_hbm,
    down_hbm,
    out_ref,
    dgrad_ref,
    ugrad_ref,
    wo,
    gate,
    down,
    xbuf,
    gbuf,
    part,
    rs_in,
    opart,
    core_in,
    y_in,
    oz_in,
    acc_p,
    acc_g,
    low,
    act,
    gpre,
    att,
    hid,
    fac,
    wbuf,
    wcol,
    load_sem,
    ag_send,
    ag_recv,
    rs_send,
    rs_recv,
    core_send,
    core_recv,
    y_send,
    y_recv,
    oz_send,
    oz_recv,
    f_send,
    f_recv,
    w_send,
    w_recv,
):
    f32 = jnp.float32
    bf16 = jnp.bfloat16
    grp = lax.axis_index("group")
    r = lax.axis_index("route")
    c = lax.axis_index("cuts")
    core = r % 2
    chip = r // 2
    r_core = chip * 2 + (1 - core)
    r_y = (1 - chip) * 2 + core
    r_diag = (1 - chip) * 2 + (1 - core)
    rows, cols = res_ref.shape

    def rslice(s):
        return pl.ds(pl.multiple_of(s * rows, rows), rows)

    def cslice(j):
        return pl.ds(pl.multiple_of(j * cols, cols), cols)

    def remote(src, dst, ss, rs, dr, dc):
        return pltpu.make_async_remote_copy(
            src_ref=src,
            dst_ref=dst,
            send_sem=ss,
            recv_sem=rs,
            device_id=(grp, dr, dc),
            device_id_type=MESH,
        )

    barrier = pltpu.get_barrier_semaphore()
    for d in range(1, n_r):
        pl.semaphore_signal(
            barrier, inc=1, device_id=(grp, (r + d) % n_r, c), device_id_type=MESH
        )
    for d in range(1, n_c):
        pl.semaphore_signal(
            barrier, inc=1, device_id=(grp, r, (c + d) % n_c), device_id_type=MESH
        )

    def slot_of(t):
        k = n_c - 1 - t // 2
        j = jnp.where(t % 2 == 0, c + k, c - k)
        return k, j, (j >= 0) & (j < n_c) & ((k > 0) | (t % 2 == 0))

    n_slots = 2 * n_c - 1

    def wo_copy(j):
        return pltpu.make_async_copy(
            wo_hbm.at[:, cslice(j)], wo.at[:, cslice(j)], load_sem.at[j]
        )

    def each_slot(body):
        def step(t, carry):
            k, j, ok = slot_of(t)

            @pl.when(ok)
            def _():
                body(k, j)

            return carry

        lax.fori_loop(0, n_slots, step, 0)

    each_slot(lambda k, j: wo_copy(j).start())
    down_copy = pltpu.make_async_copy(down_hbm, down, load_sem.at[n_c])
    gate_copy = pltpu.make_async_copy(gate_hbm, gate, load_sem.at[n_c + 1])
    down_copy.start()
    gate_copy.start()

    gbuf[c, rslice(r)] = cot_ref[...]
    wbuf[r] = wt_ref[...]
    pl.semaphore_wait(barrier, n_r - 1 + n_c - 1)

    def ag(kind, buf, what, j, s, dr, dc):
        place = buf.at[j, rslice(s)]
        return remote(
            place, place, ag_send.at[kind, what, j], ag_recv.at[kind, j, s], dr, dc
        )

    def up(kind, buf, j):
        return ag(kind, buf, 0, j, r, r, jnp.minimum(c + 1, n_c - 1))

    def dn(kind, buf, j):
        return ag(kind, buf, 1, j, r, r, jnp.maximum(c - 1, 0))

    def across(kind, buf, j):
        return ag(kind, buf, 2, j, r, r_y, c)

    def own_core(kind, buf, j):
        return ag(kind, buf, 3, j, r, r_core, c)

    def fwd_core(kind, buf, j):
        return ag(kind, buf, 4, j, r_y, r_core, c)

    def arrived(kind, buf, j, s):
        ag(kind, buf, 0, j, s, r_core, c).wait_recv()

    def spread(kind, buf, j):
        across(kind, buf, j).start()

        @pl.when((j <= c) & (c < n_c - 1))
        def _():
            up(kind, buf, j).start()

        @pl.when((j >= c) & (c > 0))
        def _():
            dn(kind, buf, j).start()

        own_core(kind, buf, j).start()

    def both_sides(k, body):
        @pl.when(c - k >= 0)
        def _():
            body(c - k)

        @pl.when((c + k < n_c) & (k > 0))
        def _():
            body(c + k)

    def z_stage(kind, buf, k):
        def one(j):
            arrived(kind, buf, j, r)
            spread(kind, buf, j)

        both_sides(k, one)

    def y_stage(kind, buf, k):
        def one(j):
            arrived(kind, buf, j, r_y)
            fwd_core(kind, buf, j).start()

        both_sides(k, one)

    def c_stage(kind, buf, k, body):
        def step(side, carry):
            j = jnp.where(side == 0, c - k, c + k)

            @pl.when((j >= 0) & (j < n_c) & ((k > 0) | (side == 0)))
            def _():
                arrived(kind, buf, j, r_core)
                arrived(kind, buf, j, r_diag)
                body(j)

            return carry

        lax.fori_loop(0, 2, step, 0)

    def ag_finish(kind, buf):
        def step(j, carry):
            across(kind, buf, j).wait_send()

            @pl.when((j <= c) & (c < n_c - 1))
            def _():
                up(kind, buf, j).wait_send()

            @pl.when((j >= c) & (c > 0))
            def _():
                dn(kind, buf, j).wait_send()

            own_core(kind, buf, j).wait_send()
            fwd_core(kind, buf, j).wait_send()
            return carry

        lax.fori_loop(0, n_c, step, 0)

    spread(0, gbuf, c)

    def w_copy(d):
        return remote(
            wbuf.at[r], wbuf.at[r], w_send.at[d], w_recv.at[r], (r + d) % n_r, c
        )

    for d in range(1, n_r):
        w_copy(d).start()

    kv_heads = k_ref.shape[1] // HEAD_DIM
    heads = q_ref.shape[1] // HEAD_DIM
    future = lax.broadcasted_iota(jnp.int32, (rows, rows), 1) > lax.broadcasted_iota(
        jnp.int32, (rows, rows), 0
    )
    for h in range(heads):
        g = h // (heads // kv_heads)
        sc = lax.dot_general(
            q_ref[:, h * HEAD_DIM : (h + 1) * HEAD_DIM],
            k_ref[:, g * HEAD_DIM : (g + 1) * HEAD_DIM],
            NT,
            preferred_element_type=f32,
        ) / math.sqrt(HEAD_DIM)
        sc = jnp.where(future, -jnp.inf, sc)
        ex = jnp.exp(sc - jnp.max(sc, axis=-1, keepdims=True))
        wts = (ex / jnp.sum(ex, axis=-1, keepdims=True)).astype(bf16)
        att[:, h * HEAD_DIM : (h + 1) * HEAD_DIM] = jnp.dot(
            wts,
            v_ref[:, g * HEAD_DIM : (g + 1) * HEAD_DIM],
            preferred_element_type=f32,
        ).astype(bf16)

    def line_copy(buf_at, inbox, ss, rs, j, upward):
        dc = jnp.minimum(c + 1, n_c - 1) if upward else jnp.maximum(c - 1, 0)
        side = 0 if upward else 1
        return remote(buf_at(j), inbox.at[side, j], ss.at[j], rs.at[side, j], r, dc)

    def line_step(buf_at, load, store, inbox, ss, rs, j):
        @pl.when(j > c)
        def _():
            @pl.when(c > 0)
            def _():
                line_copy(buf_at, inbox, ss, rs, j, True).wait_recv()
                store(j, load(j) + inbox[0, j].astype(f32))

            @pl.when(j < n_c - 1)
            def _():
                line_copy(buf_at, inbox, ss, rs, j + 1, True).wait_send()

            line_copy(buf_at, inbox, ss, rs, j, True).start()

        @pl.when(j < c)
        def _():
            @pl.when(c < n_c - 1)
            def _():
                line_copy(buf_at, inbox, ss, rs, j, False).wait_recv()
                store(j, load(j) + inbox[1, j].astype(f32))

            @pl.when(j > 0)
            def _():
                line_copy(buf_at, inbox, ss, rs, j - 1, False).wait_send()

            line_copy(buf_at, inbox, ss, rs, j, False).start()

    def line_final(buf_at, inbox, ss, rs, total):
        @pl.when(c > 0)
        def _():
            line_copy(buf_at, inbox, ss, rs, c, True).wait_recv()
            total[...] += inbox[0, c].astype(f32)

        @pl.when(c < n_c - 1)
        def _():
            line_copy(buf_at, inbox, ss, rs, c, False).wait_recv()
            total[...] += inbox[1, c].astype(f32)

    def line_finish(buf_at, inbox, ss, rs):
        @pl.when(c < n_c - 1)
        def _():
            line_copy(buf_at, inbox, ss, rs, c + 1, True).wait_send()

        @pl.when(c > 0)
        def _():
            line_copy(buf_at, inbox, ss, rs, c - 1, False).wait_send()

    def part_at(j):
        return part.at[j]

    def part_load(j):
        return part[j].astype(f32)

    def part_store(j, value):
        part[j] = value.astype(bf16)

    def project(j):
        wo_copy(j).wait()
        return jnp.dot(att[...], wo[:, cslice(j)], preferred_element_type=f32)

    def rs_loop(i, carry):
        k = n_c - 1 - i

        def side_step(side, carry2):
            j = jnp.where(side == 0, c + k, c - k)

            @pl.when((j >= 0) & (j < n_c))
            def _():
                part[j] = project(j).astype(bf16)
                line_step(part_at, part_load, part_store, rs_in, rs_send, rs_recv, j)

            return carry2

        lax.fori_loop(0, 2, side_step, 0)
        z_stage(0, gbuf, i + 1)
        return carry

    lax.fori_loop(0, n_c - 1, rs_loop, 0)
    hid[...] = res_ref[...].astype(f32) + project(c)
    line_final(part_at, rs_in, rs_send, rs_recv, hid)
    xbuf[c, rslice(r)] = hid[...].astype(bf16)
    spread(1, xbuf, c)
    lax.fori_loop(0, n_c, lambda i, z: (y_stage(0, gbuf, i), z)[1], 0)

    acc_p[...] = jnp.zeros_like(acc_p)
    acc_g[...] = jnp.zeros_like(acc_g)
    low[...] = jnp.zeros_like(low)
    half = 2 * rows
    n_half = n_r // 2

    def grad_mm(j):
        def step(m, carry):
            at = pl.ds(pl.multiple_of(m * half, half), half)
            acc_g[at] += lax.dot_general(
                gbuf[j, at], down[:, cslice(j)], NT, preferred_element_type=f32
            )
            return carry

        lax.fori_loop(0, n_half, step, 0)

    def gate_mm(j):
        def step(m, carry):
            at = pl.ds(pl.multiple_of(m * half, half), half)
            x = xbuf[j, at]
            acc_p[at] += lax.dot_general(
                x, gate[:, cslice(j)], NT, preferred_element_type=f32
            )
            low[at] += lax.dot_general(
                x, adn_ref[:, cslice(j)], NT, preferred_element_type=f32
            )
            return carry

        lax.fori_loop(0, n_half, step, 0)

    down_copy.wait()
    gate_copy.wait()

    def hidden_loop(i, carry):
        @pl.when(i <= n_c - 2)
        def _():
            z_stage(1, xbuf, i + 1)

        @pl.when(i <= n_c - 1)
        def _():
            c_stage(0, gbuf, i, grad_mm)
            y_stage(1, xbuf, i)

        @pl.when(i >= 1)
        def _():
            c_stage(1, xbuf, i - 1, gate_mm)

        return carry

    lax.fori_loop(0, n_c + 1, hidden_loop, 0)

    for d in range(1, n_r):
        src = (r + d) % n_r
        remote(
            wbuf.at[src], wbuf.at[src], w_send.at[d], w_recv.at[src], src, c
        ).wait_recv()

    eye = lax.broadcasted_iota(jnp.int32, (rows, rows), 1) == lax.broadcasted_iota(
        jnp.int32, (rows, rows), 0
    )
    mine = lax.broadcasted_iota(jnp.int32, wt_ref.shape, 0) == r

    def act_step(i, carry):
        s = (1 - chip) * 2 + i
        s = jnp.where(s >= n_r, s - n_r, s)
        at = rslice(s)
        w_row = jnp.sum(jnp.where(mine, wbuf[s], 0.0), axis=0, keepdims=True)
        w = jnp.sum(jnp.where(eye, w_row, 0.0), axis=1, keepdims=True)
        wcol[at] = jnp.broadcast_to(w, (rows, wcol.shape[1]))
        z = acc_p[at] + ADAPTER_SCALE * jnp.dot(
            low[at].astype(bf16), aup_ref[...], preferred_element_type=f32
        )
        sig = 1.0 / (1.0 + jnp.exp(-z))
        act[at] = (z * sig).astype(bf16)
        gpre[at] = (acc_g[at] * w * (sig * (1.0 + z * (1.0 - sig)))).astype(bf16)
        return carry

    lax.fori_loop(0, n_r, act_step, 0)

    def out_mm(j, base):
        at = pl.ds(pl.multiple_of(base * rows, rows), half)
        prod = jnp.dot(act[at], down[:, cslice(j)], preferred_element_type=f32)
        opart[j, at] = (prod * wcol[at, 0:1]).astype(bf16)

    def core_copy(which, j, s):
        return remote(
            opart.at[j, rslice(s)],
            core_in.at[which, j],
            core_send.at[which, j],
            core_recv.at[which, j],
            r_core,
            c,
        )

    def y_copy(j):
        return remote(
            opart.at[j, rslice(r_y)], y_in.at[j], y_send.at[j], y_recv.at[j], r_y, c
        )

    def other_mm(k, j):
        out_mm(j, (1 - chip) * 2)
        core_copy(0, j, r_diag).start()

    def far(i):
        below = jnp.minimum(c, n_c - 1 - c)
        single = n_c - 1 - 2 * below
        d = n_c - 1 - below - i
        one_side = jnp.where(c < n_c - 1 - c, c + d, c - d)
        e = i - single
        kk = below - e // 2
        two_side = jnp.where(e % 2 == 0, c + kk, c - kk)
        return jnp.where(i >= single, two_side, one_side)

    def other_pair(i):
        j = far(i)
        core_copy(0, j, r_diag).wait_recv()
        at = rslice(r_y)
        opart[j, at] = (opart[j, at].astype(f32) + core_in[0, j].astype(f32)).astype(bf16)
        y_copy(j).start()

    each_slot(other_mm)
    for i in range(AHEAD):
        other_pair(i)

    fac[c] = lax.dot_general(
        aup_ref[...], gpre[...], NT, preferred_element_type=f32
    ).astype(bf16)

    def f_copy(d, owner):
        return remote(
            fac.at[owner], fac.at[owner], f_send.at[d], f_recv.at[owner], r, (c + d) % n_c
        )

    for d in range(1, n_c):
        f_copy(d, c).start()

    def own_mm(k, j):
        out_mm(j, chip * 2)
        core_copy(1, j, r_core).start()

    each_slot(own_mm)

    ugrad_ref[...] = ADAPTER_SCALE * jnp.dot(
        low[...].T.astype(bf16), gpre[...], preferred_element_type=f32
    )
    for d in range(1, n_c):
        f_copy(d, (c + d) % n_c).wait_recv()
    total_f = fac[0].astype(f32)
    for d in range(1, n_c):
        total_f = total_f + fac[d].astype(f32)
    dgrad_ref[...] = ADAPTER_SCALE * jnp.dot(
        total_f.astype(bf16), xbuf[c], preferred_element_type=f32
    )

    def out_at(j):
        return opart.at[j, rslice(r)]

    def out_load(j):
        return opart[j, rslice(r)].astype(f32)

    def out_store(j, value):
        opart[j, rslice(r)] = value.astype(bf16)

    def route_total(j):
        core_copy(1, j, r_core).wait_recv()
        y_copy(j).wait_recv()
        return out_load(j) + core_in[1, j].astype(f32) + y_in[j].astype(f32)

    def reduce_loop(i, carry):
        j = far(i)
        out_store(j, route_total(j))
        @pl.when(i + AHEAD < n_c)
        def _():
            other_pair(i + AHEAD)

        line_step(out_at, out_load, out_store, oz_in, oz_send, oz_recv, j)
        return carry

    lax.fori_loop(0, n_c - 1, reduce_loop, 0)
    hid[...] = xbuf[c, rslice(r)].astype(f32) + route_total(c)
    line_final(out_at, oz_in, oz_send, oz_recv, hid)
    out_ref[...] = hid[...].astype(bf16)

    ag_finish(0, gbuf)
    ag_finish(1, xbuf)
    line_finish(part_at, rs_in, rs_send, rs_recv)
    line_finish(out_at, oz_in, oz_send, oz_recv)
    for d in range(1, n_r):
        w_copy(d).wait_send()
    for d in range(1, n_c):
        f_copy(d, c).wait_send()

    def last(j, carry):
        core_copy(0, j, r_diag).wait_send()
        core_copy(1, j, r_core).wait_send()
        y_copy(j).wait_send()
        return carry

    lax.fori_loop(0, n_c, last, 0)


def scratch_list(n_r, n_c, rows, cols, inner, units, rank, w_rows):
    bf16 = jnp.bfloat16
    f32 = jnp.float32
    dma = pltpu.SemaphoreType.DMA
    width = n_c * cols
    tokens = n_r * rows
    return [
        pltpu.VMEM((inner, width), bf16),
        pltpu.VMEM((units, width), bf16),
        pltpu.VMEM((units, width), bf16),
        pltpu.VMEM((n_c, tokens, cols), bf16),
        pltpu.VMEM((n_c, tokens, cols), bf16),
        pltpu.VMEM((n_c, rows, cols), bf16),
        pltpu.VMEM((2, n_c, rows, cols), bf16),
        pltpu.VMEM((n_c, tokens, cols), bf16),
        pltpu.VMEM((2, n_c, rows, cols), bf16),
        pltpu.VMEM((n_c, rows, cols), bf16),
        pltpu.VMEM((2, n_c, rows, cols), bf16),
        pltpu.VMEM((tokens, units), f32),
        pltpu.VMEM((tokens, units), f32),
        pltpu.VMEM((tokens, rank), f32),
        pltpu.VMEM((tokens, units), bf16),
        pltpu.VMEM((tokens, units), bf16),
        pltpu.VMEM((rows, inner), bf16),
        pltpu.VMEM((rows, cols), f32),
        pltpu.VMEM((n_c, rank, tokens), bf16),
        pltpu.VMEM((n_r, w_rows, rows), f32),
        pltpu.VMEM((tokens, 128), f32),
        dma((n_c + 2,)),
        dma((2, 5, n_c)),
        dma((2, n_c, n_r)),
        dma((n_c,)),
        dma((2, n_c)),
        dma((2, n_c)),
        dma((2, n_c)),
        dma((n_c,)),
        dma((n_c,)),
        dma((n_c,)),
        dma((2, n_c)),
        dma((n_c,)),
        dma((n_c,)),
        dma((n_r,)),
        dma((n_r,)),
    ]


def settle(*refs):
    for src, dst in zip(refs[:3], refs[3:]):
        dst[...] = src[...]


def dense_tokens(n_r, n_c, *args):
    (q, k, v, wo, res, cot, choices, _, router, gate, down, adn, aup) = args
    rows, cols = res.shape
    units = gate.shape[1]
    rank = adn.shape[1]
    w_rows = -(-n_r // 8) * 8
    hits = choices.T[:, None, :] == jnp.arange(w_rows, dtype=jnp.int32)[None, :, None]
    wt = jnp.sum(jnp.where(hits, router.T[:, None, :], 0.0), axis=0)
    vmem = pl.BlockSpec(memory_space=pltpu.VMEM)
    hbm = pl.BlockSpec(memory_space=pltpu.HBM)
    tokens = n_r * rows
    outs = pl.pallas_call(
        functools.partial(fused_kernel, n_r, n_c),
        out_shape=(
            jax.ShapeDtypeStruct((rows, cols), jnp.bfloat16),
            jax.ShapeDtypeStruct((rank, cols), jnp.float32),
            jax.ShapeDtypeStruct((rank, units), jnp.float32),
        ),
        in_specs=[vmem] * 8 + [hbm] * 3,
        out_specs=(vmem, vmem, vmem),
        scratch_shapes=scratch_list(
            n_r, n_c, rows, cols, q.shape[1], units, rank, w_rows
        ),
        compiler_params=pltpu.CompilerParams(
            collective_id=0, has_side_effects=True, vmem_limit_bytes=VMEM_GRANT
        ),
        cost_estimate=pl.CostEstimate(
            flops=6 * tokens * units * cols * n_c,
            bytes_accessed=2 * (q.shape[1] + 2 * units) * cols * n_c,
            transcendentals=tokens * units,
        ),
    )(q, k, v, res, cot, wt, adn[0], aup[0], wo, gate[0], down[0])
    outs = pl.pallas_call(
        settle,
        out_shape=[jax.ShapeDtypeStruct(o.shape, o.dtype) for o in outs],
        in_specs=[vmem] * 3,
        out_specs=[vmem] * 3,
    )(*outs)
    return outs[0], outs[1][None], outs[2][None]


def local(n_r, n_c, *args):
    length = args[4].shape[0]
    capacity = 4 * length // n_r
    if capacity == length and n_r == 2 * 2:
        return dense_tokens(n_r, n_c, *args)
    return exchanged_slots(*args)


def solution(mesh):
    return jax.shard_map(
        functools.partial(local, mesh.shape["route"], mesh.shape["cuts"]),
        mesh=mesh,
        in_specs=(
            P(("group", "route"), "cuts"),
            P(("group", "route"), "cuts"),
            P(("group", "route"), "cuts"),
            P("cuts", None),
            P(("group", "route"), "cuts"),
            P(("group", "route"), "cuts"),
            P(("group", "route"), None),
            P(("group", "route"), None),
            P(("group", "route"), None),
            P("route", "cuts", None),
            P("route", "cuts", None),
            P("route", None, None),
            P("route", None, "cuts"),
        ),
        out_specs=(
            P(("group", "route"), "cuts"),
            P(("group", "route"), None, "cuts"),
            P(("group", "route"), None, "cuts"),
        ),
        check_vma=False,
    )
```
